32 devices in a mesh: groups: 2 (over x), lat: 16 (over z, y, core).
Axes of the slice: x: 2, y: 2, z: 4, core: 2. Of those that a mesh axis runs over, the one named last changes fastest.
Arguments:
- field: bfloat16 [64, 128, 2688], P(('groups', 'lat')), parts along dimension 0, may hold values from -6 to 6
- target: bfloat16 [64, 128, 2688], P(('groups', 'lat')), parts along dimension 0, may hold values from -6 to 6
- cycle_len: int32 [32], replicated, may hold values from 20 to 2568, as said below
- legendre: bfloat16 [640, 32, 640], P('lat'), may hold values from -1 to 1
- spectral_filter: float32 [640, 128], replicated, may hold values from -4 to 4
Outputs:
- errors: bfloat16 [64, 128, 2688], P(('groups', 'lat')), parts along dimension 0
- grad_filter: float32 [1280, 128], P('groups'), parts along dimension 0
The draws below stay inside these ranges and needn't reach their ends.
There are 2 independent parts, one for each index of `groups`. The reference program is written for one: setup_inputs(seed, part) draws one part's arguments, and reference() takes and returns one part's arrays. A program takes and returns all parts, laid end to end along the dimension named above; an argument that names none is the same for every part. Nothing has to cross between parts.
Inputs may be any that keep to these rules, and one draw needn't show every extreme that they name: `cycle_len`: the cycles nearest the equator have exactly 2568 points and the polar cycles 20; every length is 20 plus a multiple of 4, and lengths fall from the equator toward both poles but for small steps.
All inputs are finite; a program needn't handle non-finite values.
Results may differ from the reference program's by a relative error of at most 0.0079.
Values may be sent and summed in bfloat16 or wider, within the bound.
A program may use at most 256 MiB of HBM per device.

```python
import math
import jax
import jax.numpy as jnp
from jax import lax

C = 128
MM = 640
LL = 640
CYCLE_MAX = 2568
LPAD = 2688
HALF = 1288
NRING = 32


def draw_cycle_len(key, part):
    key = jax.random.fold_in(key, 11)
    cycles_all = jnp.arange(NRING, dtype=jnp.int32)
    from_pole = jnp.minimum(cycles_all, NRING - 1 - cycles_all)
    halfway = NRING // 2
    base_len = 20 + 4 * ((CYCLE_MAX - 20) // 4 * from_pole // max(halfway - 1, 1))
    jitter = 4 * jax.random.randint(key, (NRING,), 0, 3)
    jitter = jnp.where(from_pole == halfway - 1, 0, jitter)
    return jnp.maximum(base_len - jitter, 20).astype(jnp.int32)


def level_of(rng, dims, pieces, smallest, top_value):
    gain = 1.0
    for axis_at, shards_of in pieces:
        steps = jax.random.uniform(jax.random.fold_in(jax.random.fold_in(rng, 6), axis_at), (shards_of,), jnp.float32, smallest / len(pieces), top_value / len(pieces))
        gain = gain * jnp.repeat(jnp.exp(steps), dims[axis_at] // shards_of).reshape((-1,) + (1,) * (len(dims) - 1 - axis_at))
    return gain


def scatter_about(own_key, dims, scale, limit, cuts=(), kind=jnp.bfloat16):
    drawn = jax.random.normal(own_key, dims, jnp.float32) * scale
    if len(cuts) > 0:
        drawn = level_of(own_key, dims, cuts, -0.22, 0.18) * drawn
    return jnp.clip(drawn, min=-limit, max=limit).astype(kind)


def setup_inputs(seed: int = 0, part: int = 0) -> dict:
    streams_of = jax.random.split(jax.random.key(seed), 6)
    own_keys = jax.random.split(jax.random.fold_in(streams_of[5], part), 6)
    field = scatter_about(own_keys[0], (NRING, C, LPAD), 1.0, 6.0, ((0, 16),))
    target = scatter_about(own_keys[1], (NRING, C, LPAD), 1.0, 6.0, ((0, 16),))
    cycle_len = draw_cycle_len(jax.random.fold_in(streams_of[5], 71), part)
    legendre = scatter_about(streams_of[3], (MM, NRING, LL), NRING ** -0.5, 1.0, ((0, 16),))
    spectral_filter = scatter_about(streams_of[4], (LL, C), 1.0, 4.0, (), jnp.float32)
    return dict(field=field, target=target, cycle_len=cycle_len, legendre=legendre, spectral_filter=spectral_filter)


def fold_table(length, first_col, amount, upper_col):
    columns = first_col + jnp.arange(amount, dtype=jnp.int32)
    wavenum = jnp.arange(MM, dtype=jnp.int32)
    half_len = length // 2
    phases = (wavenum[:, None] * columns[None, :]) % length
    angles = (2.0 * math.pi) * phases.astype(jnp.float32) / length.astype(jnp.float32)
    inside = (columns[None, :] < upper_col) & (columns[None, :] <= half_len) & (wavenum[:, None] < half_len)
    cosine = jnp.where(inside, jnp.cos(angles), 0.0).astype(jnp.bfloat16)
    sine_part = jnp.where(inside, jnp.sin(angles), 0.0).astype(jnp.bfloat16)
    return jnp.stack([cosine, sine_part])


def mirror_cols(values, length, width_out):
    blank = jnp.zeros((values.shape[0], width_out), values.dtype)
    extended = jnp.concatenate([blank, values[:, ::-1], blank], axis=1)
    start_col = (width_out + values.shape[1] - 1 - length).astype(jnp.int32)
    return lax.dynamic_slice_in_dim(extended, start_col, width_out, 1)


def fold_cycle(values, length):
    half_len = length // 2
    direct = values[:, :HALF].astype(jnp.float32)
    mirrored = mirror_cols(values, length, HALF).astype(jnp.float32)
    col_index = jnp.arange(HALF, dtype=jnp.int32)[None, :]
    middle = (col_index >= 1) & (col_index < half_len)
    rim_cols = (col_index == 0) | (col_index == half_len)
    even_part = jnp.where(middle, direct + mirrored, jnp.where(rim_cols, direct, 0.0)).astype(jnp.bfloat16)
    odd_part = jnp.where(middle, direct - mirrored, 0.0).astype(jnp.bfloat16)
    return even_part, odd_part


def unfold_cycle(cos_part, sin_part, length):
    half_len = length // 2
    front_part = jnp.concatenate([cos_part - sin_part, jnp.zeros((cos_part.shape[0], LPAD - HALF), cos_part.dtype)], axis=1)
    mirrored = mirror_cols(cos_part + sin_part, length, LPAD)
    columns = jnp.arange(LPAD, dtype=jnp.int32)[None, :]
    return jnp.where(columns <= half_len, front_part, jnp.where(columns < length, mirrored, 0.0))


def reference(field, target, cycle_len, legendre, spectral_filter):
    sign_pair = jnp.array([1.0, -1.0], dtype=jnp.float32)[:, None, None]
    wavenum = jnp.arange(MM, dtype=jnp.int32)
    doubled = jnp.where(wavenum == 0, 1.0, 2.0).astype(jnp.float32)[None, :, None]
    degrees = jnp.arange(LL, dtype=jnp.int32)
    columns = jnp.arange(LPAD, dtype=jnp.int32)

    def analyse(values, length, cycle_tab):
        even_part, odd_part = fold_cycle(values, length)
        cos_sum = jnp.einsum('mk,ck->mc', cycle_tab[0], even_part.astype(jnp.float32))
        sin_sum = jnp.einsum('mk,ck->mc', cycle_tab[1], odd_part.astype(jnp.float32))
        return jnp.stack([cos_sum, sin_sum])

    def analyse_cycle(inputs):
        values, length = inputs
        cycle_tab = fold_table(length, 0, HALF, HALF).astype(jnp.float32)
        totals = analyse(values, length, cycle_tab)
        return (totals * sign_pair / length.astype(jnp.float32)).astype(jnp.bfloat16)

    coeffs = lax.map(analyse_cycle, (field, cycle_len))
    coeff_modes = jnp.transpose(coeffs, (2, 0, 1, 3)).reshape(MM, NRING, 2 * C)

    def forward_mode(inputs):
        weights, values, wave = inputs
        amplitude = jnp.dot(weights.T, values, preferred_element_type=jnp.float32).reshape(LL, 2, C)
        keeper = (degrees >= wave).astype(jnp.float32)[:, None, None]
        filtered = (amplitude * (keeper * spectral_filter[:, None, :])).astype(jnp.bfloat16).reshape(LL, 2 * C)
        return jnp.dot(weights, filtered, preferred_element_type=jnp.float32).astype(jnp.bfloat16)

    synth_modes = lax.map(forward_mode, (legendre, coeff_modes, wavenum))
    synth = synth_modes.reshape(MM, NRING, 2, C).transpose(1, 2, 0, 3)

    def error_cycle(inputs):
        values, wanted, length = inputs
        cycle_tab = fold_table(length, 0, HALF, HALF).astype(jnp.float32)
        weighted = values.astype(jnp.float32) * doubled
        cos_part = jnp.einsum('mc,mk->ck', weighted[0], cycle_tab[0])
        sin_part = jnp.einsum('mc,mk->ck', weighted[1], cycle_tab[1])
        output = unfold_cycle(cos_part, sin_part, length)
        errors = jnp.where(columns[None, :] < length, output - wanted.astype(jnp.float32), 0.0).astype(jnp.bfloat16)
        totals = analyse(errors, length, cycle_tab)
        return errors, (totals * sign_pair * doubled).astype(jnp.bfloat16)

    errors, grad_coeffs = lax.map(error_cycle, (synth, target, cycle_len))
    grad_modes_in = jnp.transpose(grad_coeffs, (2, 0, 1, 3)).reshape(MM, NRING, 2 * C)

    def backward_mode(carry_sum, inputs):
        weights, values, grad_values, wave = inputs
        amplitude = jnp.dot(weights.T, values, preferred_element_type=jnp.float32).reshape(LL, 2, C)
        grad_amp = jnp.dot(weights.T, grad_values, preferred_element_type=jnp.float32).reshape(LL, 2, C)
        keeper = (degrees >= wave).astype(jnp.float32)[:, None, None]
        return carry_sum + jnp.sum(amplitude * grad_amp * keeper, axis=1), None

    grad_filter, unused_out = lax.scan(backward_mode, jnp.zeros((LL, C), jnp.float32), (legendre, coeff_modes, grad_modes_in, wavenum))
    return errors, grad_filter
```

```python
import math

import jax
import jax.numpy as jnp
from jax import lax
from jax.sharding import PartitionSpec as P

COARSE = 32


def turn_rows(length, waves, col_count):
    columns = jnp.arange(col_count, dtype=jnp.int32)
    product = (waves[:, None] * columns[None, :]).astype(jnp.float32)
    len_f = length.astype(jnp.float32)
    inverse = 1.0 / len_f
    rest = product - jnp.round(product * inverse) * len_f
    half_angle = (math.pi * inverse) * rest
    square = half_angle * half_angle
    cos_half = jnp.ones_like(square)
    sin_half = jnp.ones_like(square)
    for order in range(6, 0, -1):
        cos_half = 1.0 - square * cos_half * (1.0 / ((2 * order - 1) * (2 * order)))
        sin_half = 1.0 - square * sin_half * (1.0 / ((2 * order) * (2 * order + 1)))
    sin_half = sin_half * half_angle
    return 1.0 - 2.0 * sin_half * sin_half, 2.0 * sin_half * cos_half


def local(field, target, cycle_len, legendre, spectral_filter):
    cycle_count, chan_count, col_count = field.shape
    mode_local, ring_count, degree_count = legendre.shape
    devices = ring_count // cycle_count
    mode_count = mode_local * devices
    position = lax.axis_index("lat")
    own_len = lax.dynamic_slice_in_dim(cycle_len, position * cycle_count, cycle_count)
    wavenum = jnp.arange(mode_count, dtype=jnp.int32)
    doubled = jnp.where(wavenum == 0, 1.0, 2.0).astype(jnp.float32)
    live_modes = (wavenum[None, :] < (own_len // 2)[:, None]).astype(jnp.float32)
    weight_modes = (live_modes * doubled[None])[:, None, :, None]
    columns = jnp.arange(col_count, dtype=jnp.int32)
    live_cols = (columns[None, :] < own_len[:, None])[:, None, :]

    coarse_waves = COARSE * jnp.arange(mode_count // COARSE, dtype=jnp.int32)
    fine_waves = jnp.arange(COARSE, dtype=jnp.int32)
    coarse = [turn_rows(own_len[i], coarse_waves, col_count) for i in range(cycle_count)]
    fine = [turn_rows(own_len[i], fine_waves, col_count) for i in range(cycle_count)]
    coarse, fine = lax.optimization_barrier((coarse, fine))
    tables = []
    for (cos_a, sin_a), (cos_b, sin_b) in zip(coarse, fine):
        cos_a, sin_a = cos_a[:, None, :], sin_a[:, None, :]
        cos_b, sin_b = cos_b[None], sin_b[None]
        cosine = (cos_a * cos_b - sin_a * sin_b).astype(jnp.bfloat16)
        minus_sine = (-(sin_a * cos_b) - cos_a * sin_b).astype(jnp.bfloat16)
        tables.append(
            [
                cosine.reshape(mode_count, col_count),
                minus_sine.reshape(mode_count, col_count),
            ]
        )
    tables = lax.optimization_barrier(tables)

    def analyse(values):
        return jnp.stack(
            [
                jnp.stack(
                    [
                        jnp.einsum("mj,cj->mc", tab, values[i], preferred_element_type=jnp.float32)
                        for tab in tables[i]
                    ]
                )
                for i in range(cycle_count)
            ]
        )

    live_field = jnp.where(live_cols, field, jnp.zeros_like(field))
    scale = live_modes[:, None, :, None] / own_len.astype(jnp.float32)[:, None, None, None]
    coeffs = (analyse(live_field) * scale).astype(jnp.bfloat16)
    gathered = lax.all_to_all(coeffs, "lat", split_axis=2, concat_axis=0, tiled=True)

    mode_ids = position * mode_local + jnp.arange(mode_local, dtype=jnp.int32)
    degrees = jnp.arange(degree_count, dtype=jnp.int32)
    keeper = (degrees[None, :] >= mode_ids[:, None]).astype(jnp.float32)[:, :, None, None]
    gain_table = keeper * spectral_filter[None, :, None, :]
    amplitude = jnp.einsum("mrl,rpmc->mlpc", legendre, gathered, preferred_element_type=jnp.float32)
    filtered = (amplitude * gain_table).astype(jnp.bfloat16)
    synth_modes = jnp.einsum(
        "mrl,mlpc->rpmc", legendre, filtered, preferred_element_type=jnp.float32
    ).astype(jnp.bfloat16)
    synth_back = lax.all_to_all(synth_modes, "lat", split_axis=0, concat_axis=2, tiled=True)

    weighted = (synth_back.astype(jnp.float32) * weight_modes).astype(jnp.bfloat16)
    output = jnp.stack(
        [
            sum(
                jnp.einsum("mc,mj->cj", weighted[i, p], tables[i][p], preferred_element_type=jnp.float32)
                for p in range(2)
            )
            for i in range(cycle_count)
        ]
    )
    errors = jnp.where(live_cols, output - target.astype(jnp.float32), 0.0).astype(jnp.bfloat16)

    grad_coeffs = (analyse(errors) * weight_modes).astype(jnp.bfloat16)
    grad_gathered = lax.all_to_all(grad_coeffs, "lat", split_axis=2, concat_axis=0, tiled=True)
    grad_amp = jnp.einsum(
        "mrl,rpmc->mlpc", legendre, grad_gathered, preferred_element_type=jnp.float32
    )
    filter_term = jnp.sum(amplitude * grad_amp * keeper, axis=(0, 2))
    pieces = filter_term.reshape(devices, degree_count // devices, chan_count)
    own_sum = jnp.sum(lax.all_to_all(pieces, "lat", split_axis=0, concat_axis=0, tiled=True), axis=0)
    spread = jnp.broadcast_to(own_sum[None], pieces.shape)
    grad_filter = lax.all_to_all(spread, "lat", split_axis=0, concat_axis=0, tiled=True)
    return (errors, grad_filter.reshape(degree_count, chan_count))


def solution(mesh):
    return jax.shard_map(
        local,
        mesh=mesh,
        in_specs=(
            P(("groups", "lat"), None, None),
            P(("groups", "lat"), None, None),
            P(),
            P("lat", None, None),
            P(),
        ),
        out_specs=(P(("groups", "lat"), None, None), P("groups", None)),
        check_vma=False,
    )
```

```python
import functools
import math

import jax
import jax.numpy as jnp
from jax import lax
from jax.experimental import pallas as pl
from jax.experimental.pallas import tpu as pltpu
from jax.sharding import PartitionSpec as P

COARSE = 32


def turn_rows(length, waves, col_count):
    columns = jnp.arange(col_count, dtype=jnp.int32)
    product = (waves[:, None] * columns[None, :]).astype(jnp.float32)
    len_f = length.astype(jnp.float32)
    inverse = 1.0 / len_f
    rest = product - jnp.round(product * inverse) * len_f
    half_angle = (math.pi * inverse) * rest
    square = half_angle * half_angle
    cos_half = jnp.ones_like(square)
    sin_half = jnp.ones_like(square)
    for order in range(6, 0, -1):
        cos_half = 1.0 - square * cos_half * (1.0 / ((2 * order - 1) * (2 * order)))
        sin_half = 1.0 - square * sin_half * (1.0 / ((2 * order) * (2 * order + 1)))
    sin_half = sin_half * half_angle
    return 1.0 - 2.0 * sin_half * sin_half, 2.0 * sin_half * cos_half


def greet_all(count, me):
    barrier = pltpu.get_barrier_semaphore()

    @pl.loop(1, count)
    def _(step):
        pl.semaphore_signal(barrier, inc=1, device_id={"lat": lax.rem(me + step, count)})

    pl.semaphore_wait(barrier, count - 1)


def send_all(count, me, source_of, landing, send_sem, recv_sem):
    @pl.loop(1, count)
    def _(step):
        peer = lax.rem(me + step, count)
        pltpu.make_async_remote_copy(
            src_ref=source_of(peer),
            dst_ref=landing.at[me],
            send_sem=send_sem.at[step],
            recv_sem=recv_sem.at[step],
            device_id={"lat": peer},
        ).start()


def wait_all(count, me, source_of, landing, send_sem, recv_sem):
    @pl.loop(1, count)
    def _(step):
        sender = lax.rem(me + count - step, count)
        peer = lax.rem(me + step, count)
        copy = pltpu.make_async_remote_copy(
            src_ref=source_of(peer),
            dst_ref=landing.at[sender],
            send_sem=send_sem.at[step],
            recv_sem=recv_sem.at[step],
            device_id={"lat": peer},
        )
        copy.wait_recv()
        copy.wait_send()


def exchange_kernel(count, x_ref, out_ref, send_sem, recv_sem):
    me = lax.axis_index("lat")
    greet_all(count, me)
    send_all(count, me, lambda peer: x_ref.at[peer], out_ref, send_sem, recv_sem)
    out_ref[me] = x_ref[me]
    wait_all(count, me, lambda peer: x_ref.at[peer], out_ref, send_sem, recv_sem)


def exchange(values, call_id):
    count, rows, width = values.shape
    padded = -(-rows // 16) * 16
    if padded != rows:
        values = jnp.pad(values, ((0, 0), (0, padded - rows), (0, 0)))
    out = pl.pallas_call(
        functools.partial(exchange_kernel, count),
        out_shape=jax.ShapeDtypeStruct(values.shape, values.dtype),
        in_specs=[pl.BlockSpec(memory_space=pltpu.VMEM)],
        out_specs=pl.BlockSpec(memory_space=pltpu.VMEM),
        scratch_shapes=[pltpu.SemaphoreType.DMA((count,)), pltpu.SemaphoreType.DMA((count,))],
        compiler_params=pltpu.CompilerParams(
            collective_id=call_id, has_side_effects=True, vmem_limit_bytes=16 * 2**20
        ),
        name=f"exchange_{call_id}",
    )(values)
    return out[:, :rows]


def total_kernel(
    count, x_ref, out_ref, landed, spread, own, send_a, recv_a, send_b, recv_b
):
    me = lax.axis_index("lat")
    rows = x_ref.shape[1]
    greet_all(count, me)
    send_all(count, me, lambda peer: x_ref.at[peer], landed, send_a, recv_a)
    landed[me] = x_ref[me]
    wait_all(count, me, lambda peer: x_ref.at[peer], landed, send_a, recv_a)
    total = jnp.sum(landed[...], axis=0)
    blank = jnp.zeros((own.shape[0] - rows, total.shape[1]), total.dtype)
    own[...] = jnp.concatenate([total, blank], axis=0).astype(own.dtype)
    send_all(count, me, lambda peer: own, spread, send_b, recv_b)
    spread[me] = own[...]
    wait_all(count, me, lambda peer: own, spread, send_b, recv_b)
    out_ref[...] = spread[...].astype(jnp.float32)[:, :rows]


def total_over(pieces, call_id):
    count, rows, width = pieces.shape
    padded = -(-rows // 16) * 16 + (16 if rows % 16 == 0 else 0)
    sems = [pltpu.SemaphoreType.DMA((count,)) for _ in range(4)]
    return pl.pallas_call(
        functools.partial(total_kernel, count),
        out_shape=jax.ShapeDtypeStruct(pieces.shape, jnp.float32),
        in_specs=[pl.BlockSpec(memory_space=pltpu.VMEM)],
        out_specs=pl.BlockSpec(memory_space=pltpu.VMEM),
        scratch_shapes=[
            pltpu.VMEM(pieces.shape, jnp.float32),
            pltpu.VMEM((count, padded, width), jnp.bfloat16),
            pltpu.VMEM((padded, width), jnp.bfloat16),
        ]
        + sems,
        compiler_params=pltpu.CompilerParams(
            collective_id=call_id, has_side_effects=True, vmem_limit_bytes=16 * 2**20
        ),
        name="total_over",
    )(pieces)


def local(field, target, cycle_len, legendre, spectral_filter):
    cycle_count, chan_count, col_count = field.shape
    mode_local, ring_count, degree_count = legendre.shape
    devices = ring_count // cycle_count
    mode_count = mode_local * devices
    position = lax.axis_index("lat")
    own_len = lax.dynamic_slice_in_dim(cycle_len, position * cycle_count, cycle_count)
    wavenum = jnp.arange(mode_count, dtype=jnp.int32)
    doubled = jnp.where(wavenum == 0, 1.0, 2.0).astype(jnp.float32)
    live_modes = (wavenum[None, :] < (own_len // 2)[:, None]).astype(jnp.float32)
    weight_modes = (live_modes * doubled[None])[:, None, :, None]
    columns = jnp.arange(col_count, dtype=jnp.int32)
    live_cols = (columns[None, :] < own_len[:, None])[:, None, :]

    coarse_waves = COARSE * jnp.arange(mode_count // COARSE, dtype=jnp.int32)
    fine_waves = jnp.arange(COARSE, dtype=jnp.int32)
    coarse = [turn_rows(own_len[i], coarse_waves, col_count) for i in range(cycle_count)]
    fine = [turn_rows(own_len[i], fine_waves, col_count) for i in range(cycle_count)]
    coarse, fine = lax.optimization_barrier((coarse, fine))
    tables = []
    for (cos_a, sin_a), (cos_b, sin_b) in zip(coarse, fine):
        cos_a, sin_a = cos_a[:, None, :], sin_a[:, None, :]
        cos_b, sin_b = cos_b[None], sin_b[None]
        cosine = (cos_a * cos_b - sin_a * sin_b).astype(jnp.bfloat16)
        minus_sine = (-(sin_a * cos_b) - cos_a * sin_b).astype(jnp.bfloat16)
        tables.append(
            [
                cosine.reshape(mode_count, col_count),
                minus_sine.reshape(mode_count, col_count),
            ]
        )
    tables = lax.optimization_barrier(tables)

    def analyse(values):
        return jnp.stack(
            [
                jnp.stack(
                    [
                        jnp.einsum("mj,cj->mc", tab, values[i], preferred_element_type=jnp.float32)
                        for tab in tables[i]
                    ]
                )
                for i in range(cycle_count)
            ]
        )

    live_field = jnp.where(live_cols, field, jnp.zeros_like(field))
    scale = live_modes[:, None, :, None] / own_len.astype(jnp.float32)[:, None, None, None]
    coeffs = (analyse(live_field) * scale).astype(jnp.bfloat16)

    def to_modes(values, call_id):
        split = values.reshape(cycle_count, 2, devices, mode_local, chan_count)
        rows = split.transpose(2, 0, 1, 3, 4).reshape(devices, -1, chan_count)
        return exchange(rows, call_id).reshape(ring_count, 2, mode_local, chan_count)

    def to_cycles(values, call_id):
        rows = exchange(values.reshape(devices, -1, chan_count), call_id)
        split = rows.reshape(devices, cycle_count, 2, mode_local, chan_count)
        return split.transpose(1, 2, 0, 3, 4).reshape(cycle_count, 2, mode_count, chan_count)

    gathered = to_modes(coeffs, 0)

    mode_ids = position * mode_local + jnp.arange(mode_local, dtype=jnp.int32)
    degrees = jnp.arange(degree_count, dtype=jnp.int32)
    kept = degrees[None, None, :] >= mode_ids[:, None, None]
    legendre = lax.optimization_barrier(jnp.where(kept, legendre, jnp.zeros_like(legendre)))
    amplitude = jnp.einsum("mrl,rpmc->mlpc", legendre, gathered, preferred_element_type=jnp.float32)
    filtered = (amplitude * spectral_filter[None, :, None, :]).astype(jnp.bfloat16)
    synth_modes = jnp.einsum(
        "mrl,mlpc->rpmc", legendre, filtered, preferred_element_type=jnp.float32
    ).astype(jnp.bfloat16)
    synth_back = to_cycles(synth_modes, 1)

    weighted = (synth_back.astype(jnp.float32) * weight_modes).astype(jnp.bfloat16)
    output = jnp.stack(
        [
            sum(
                jnp.einsum("mc,mj->cj", weighted[i, p], tables[i][p], preferred_element_type=jnp.float32)
                for p in range(2)
            )
            for i in range(cycle_count)
        ]
    )
    errors = jnp.where(live_cols, output - target.astype(jnp.float32), 0.0).astype(jnp.bfloat16)

    grad_coeffs = (analyse(errors) * weight_modes).astype(jnp.bfloat16)
    grad_gathered = to_modes(grad_coeffs, 2)
    grad_amp = jnp.einsum(
        "mrl,rpmc->mlpc", legendre, grad_gathered, preferred_element_type=jnp.float32
    )
    filter_term = jnp.sum(amplitude * grad_amp, axis=(0, 2))
    pieces = filter_term.reshape(devices, degree_count // devices, chan_count)
    grad_filter = total_over(pieces, 3)
    return (errors, grad_filter.reshape(degree_count, chan_count))


def solution(mesh):
    return jax.shard_map(
        local,
        mesh=mesh,
        in_specs=(
            P(("groups", "lat"), None, None),
            P(("groups", "lat"), None, None),
            P(),
            P("lat", None, None),
            P(),
        ),
        out_specs=(P(("groups", "lat"), None, None), P("groups", None)),
        check_vma=False,
    )
```

```python
import functools
import math

import jax
import jax.numpy as jnp
from jax import lax
from jax.experimental import pallas as pl
from jax.experimental.pallas import tpu as pltpu
from jax.sharding import PartitionSpec as P

COARSE = 32


def turn_rows(length, waves, col_count):
    columns = jnp.arange(col_count, dtype=jnp.int32)
    product = (waves[:, None] * columns[None, :]).astype(jnp.float32)
    len_f = length.astype(jnp.float32)
    inverse = 1.0 / len_f
    rest = product - jnp.round(product * inverse) * len_f
    half_angle = (math.pi * inverse) * rest
    square = half_angle * half_angle
    cos_half = jnp.ones_like(square)
    sin_half = jnp.ones_like(square)
    for order in range(6, 0, -1):
        cos_half = 1.0 - square * cos_half * (1.0 / ((2 * order - 1) * (2 * order)))
        sin_half = 1.0 - square * sin_half * (1.0 / ((2 * order) * (2 * order + 1)))
    sin_half = sin_half * half_angle
    return 1.0 - 2.0 * sin_half * sin_half, 2.0 * sin_half * cos_half


def greet_all(count, me):
    barrier = pltpu.get_barrier_semaphore()

    @pl.loop(1, count)
    def _(step):
        pl.semaphore_signal(barrier, inc=1, device_id={"lat": lax.rem(me + step, count)})

    pl.semaphore_wait(barrier, count - 1)


def send_all(count, me, source_of, landing, send_sem, recv_sem):
    @pl.loop(1, count)
    def _(step):
        peer = lax.rem(me + step, count)
        pltpu.make_async_remote_copy(
            src_ref=source_of(peer),
            dst_ref=landing.at[me],
            send_sem=send_sem.at[step],
            recv_sem=recv_sem.at[step],
            device_id={"lat": peer},
        ).start()


def wait_all(count, me, source_of, landing, send_sem, recv_sem):
    @pl.loop(1, count)
    def _(step):
        sender = lax.rem(me + count - step, count)
        peer = lax.rem(me + step, count)
        copy = pltpu.make_async_remote_copy(
            src_ref=source_of(peer),
            dst_ref=landing.at[sender],
            send_sem=send_sem.at[step],
            recv_sem=recv_sem.at[step],
            device_id={"lat": peer},
        )
        copy.wait_recv()
        copy.wait_send()


def exchange_kernel(count, x_ref, out_ref, send_sem, recv_sem):
    me = lax.axis_index("lat")
    greet_all(count, me)
    send_all(count, me, lambda peer: x_ref.at[peer], out_ref, send_sem, recv_sem)
    out_ref[me] = x_ref[me]
    wait_all(count, me, lambda peer: x_ref.at[peer], out_ref, send_sem, recv_sem)


def exchange(values, call_id):
    count, rows, width = values.shape
    padded = -(-rows // 16) * 16
    if padded != rows:
        values = jnp.pad(values, ((0, 0), (0, padded - rows), (0, 0)))
    out = pl.pallas_call(
        functools.partial(exchange_kernel, count),
        out_shape=jax.ShapeDtypeStruct(values.shape, values.dtype),
        in_specs=[pl.BlockSpec(memory_space=pltpu.VMEM)],
        out_specs=pl.BlockSpec(memory_space=pltpu.VMEM),
        scratch_shapes=[pltpu.SemaphoreType.DMA((count,)), pltpu.SemaphoreType.DMA((count,))],
        compiler_params=pltpu.CompilerParams(
            collective_id=call_id, has_side_effects=True, vmem_limit_bytes=16 * 2**20
        ),
        name=f"exchange_{call_id}",
    )(values)
    return out[:, :rows]


def total_kernel(
    count, x_ref, out_ref, landed, spread, own, send_a, recv_a, send_b, recv_b
):
    me = lax.axis_index("lat")
    rows = out_ref.shape[1]
    greet_all(count, me)
    send_all(count, me, lambda peer: x_ref.at[peer], landed, send_a, recv_a)
    landed[me] = x_ref[me]
    wait_all(count, me, lambda peer: x_ref.at[peer], landed, send_a, recv_a)
    own[...] = jnp.sum(landed[...].astype(jnp.float32), axis=0).astype(own.dtype)
    send_all(count, me, lambda peer: own, spread, send_b, recv_b)
    spread[me] = own[...]
    wait_all(count, me, lambda peer: own, spread, send_b, recv_b)
    out_ref[...] = spread[...].astype(jnp.float32)[:, :rows]


def total_over(pieces, call_id):
    count, rows, width = pieces.shape
    padded = -(-rows // 16) * 16
    terms = jnp.pad(pieces, ((0, 0), (0, padded - rows), (0, 0))).astype(jnp.bfloat16)
    sems = [pltpu.SemaphoreType.DMA((count,)) for _ in range(4)]
    return pl.pallas_call(
        functools.partial(total_kernel, count),
        out_shape=jax.ShapeDtypeStruct(pieces.shape, jnp.float32),
        in_specs=[pl.BlockSpec(memory_space=pltpu.VMEM)],
        out_specs=pl.BlockSpec(memory_space=pltpu.VMEM),
        scratch_shapes=[
            pltpu.VMEM((count, padded, width), jnp.bfloat16),
            pltpu.VMEM((count, padded, width), jnp.bfloat16),
            pltpu.VMEM((padded, width), jnp.bfloat16),
        ]
        + sems,
        compiler_params=pltpu.CompilerParams(
            collective_id=call_id, has_side_effects=True, vmem_limit_bytes=16 * 2**20
        ),
        name="total_over",
    )(terms)


def local(field, target, cycle_len, legendre, spectral_filter):
    cycle_count, chan_count, col_count = field.shape
    mode_local, ring_count, degree_count = legendre.shape
    devices = ring_count // cycle_count
    mode_count = mode_local * devices
    position = lax.axis_index("lat")
    own_len = lax.dynamic_slice_in_dim(cycle_len, position * cycle_count, cycle_count)
    wavenum = jnp.arange(mode_count, dtype=jnp.int32)
    doubled = jnp.where(wavenum == 0, 1.0, 2.0).astype(jnp.float32)
    live_modes = (wavenum[None, :] < (own_len // 2)[:, None]).astype(jnp.float32)
    weight_modes = (live_modes * doubled[None])[:, None, :, None]
    columns = jnp.arange(col_count, dtype=jnp.int32)
    live_cols = (columns[None, :] < own_len[:, None])[:, None, :]

    coarse_waves = COARSE * jnp.arange(mode_count // COARSE, dtype=jnp.int32)
    fine_waves = jnp.arange(COARSE, dtype=jnp.int32)
    coarse = [turn_rows(own_len[i], coarse_waves, col_count) for i in range(cycle_count)]
    fine = [turn_rows(own_len[i], fine_waves, col_count) for i in range(cycle_count)]
    coarse, fine = lax.optimization_barrier((coarse, fine))
    tables = []
    for (cos_a, sin_a), (cos_b, sin_b) in zip(coarse, fine):
        cos_a, sin_a = cos_a[:, None, :], sin_a[:, None, :]
        cos_b, sin_b = cos_b[None], sin_b[None]
        cosine = (cos_a * cos_b - sin_a * sin_b).astype(jnp.bfloat16)
        minus_sine = (-(sin_a * cos_b) - cos_a * sin_b).astype(jnp.bfloat16)
        tables.append(
            [
                cosine.reshape(mode_count, col_count),
                minus_sine.reshape(mode_count, col_count),
            ]
        )
    tables = lax.optimization_barrier(tables)

    def analyse(values):
        return jnp.stack(
            [
                jnp.stack(
                    [
                        jnp.einsum("mj,cj->mc", tab, values[i], preferred_element_type=jnp.float32)
                        for tab in tables[i]
                    ]
                )
                for i in range(cycle_count)
            ]
        )

    live_field = jnp.where(live_cols, field, jnp.zeros_like(field))
    scale = live_modes[:, None, :, None] / own_len.astype(jnp.float32)[:, None, None, None]
    coeffs = (analyse(live_field) * scale).astype(jnp.bfloat16)

    def to_modes(values, call_id):
        split = values.reshape(cycle_count, 2, devices, mode_local, chan_count)
        rows = split.transpose(2, 0, 1, 3, 4).reshape(devices, -1, chan_count)
        return exchange(rows, call_id).reshape(ring_count, 2, mode_local, chan_count)

    def to_cycles(values, call_id):
        rows = exchange(values.reshape(devices, -1, chan_count), call_id)
        split = rows.reshape(devices, cycle_count, 2, mode_local, chan_count)
        return split.transpose(1, 2, 0, 3, 4).reshape(cycle_count, 2, mode_count, chan_count)

    gathered = to_modes(coeffs, 0)

    mode_ids = position * mode_local + jnp.arange(mode_local, dtype=jnp.int32)
    degrees = jnp.arange(degree_count, dtype=jnp.int32)
    kept = degrees[None, None, :] >= mode_ids[:, None, None]
    legendre = lax.optimization_barrier(jnp.where(kept, legendre, jnp.zeros_like(legendre)))
    amplitude = jnp.einsum("mrl,rpmc->mlpc", legendre, gathered, preferred_element_type=jnp.float32)
    filtered = (amplitude * spectral_filter[None, :, None, :]).astype(jnp.bfloat16)
    synth_modes = jnp.einsum(
        "mrl,mlpc->rpmc", legendre, filtered, preferred_element_type=jnp.float32
    ).astype(jnp.bfloat16)
    synth_back = to_cycles(synth_modes, 1)

    weighted = (synth_back.astype(jnp.float32) * weight_modes).astype(jnp.bfloat16)
    output = jnp.stack(
        [
            sum(
                jnp.einsum("mc,mj->cj", weighted[i, p], tables[i][p], preferred_element_type=jnp.float32)
                for p in range(2)
            )
            for i in range(cycle_count)
        ]
    )
    errors = jnp.where(live_cols, output - target.astype(jnp.float32), 0.0).astype(jnp.bfloat16)

    grad_coeffs = (analyse(errors) * weight_modes).astype(jnp.bfloat16)
    grad_gathered = to_modes(grad_coeffs, 2)
    grad_amp = jnp.einsum(
        "mrl,rpmc->mlpc", legendre, grad_gathered, preferred_element_type=jnp.float32
    )
    filter_term = jnp.sum(amplitude * grad_amp, axis=(0, 2))
    pieces = filter_term.reshape(devices, degree_count // devices, chan_count)
    grad_filter = total_over(pieces, 3)
    return (errors, grad_filter.reshape(degree_count, chan_count))


def solution(mesh):
    return jax.shard_map(
        local,
        mesh=mesh,
        in_specs=(
            P(("groups", "lat"), None, None),
            P(("groups", "lat"), None, None),
            P(),
            P("lat", None, None),
            P(),
        ),
        out_specs=(P(("groups", "lat"), None, None), P("groups", None)),
        check_vma=False,
    )
```
